32 devices in a mesh: op: 2 (over core), sec: 16 (over z, y, x).
Axes of the slice: x: 2, y: 2, z: 4, core: 2. Of those that a mesh axis runs over, the one named last changes fastest.
Arguments:
- psi: float32 [32, 512, 512], P('sec'), may hold values from -6 to 6
- left_env: float32 [8, 32, 512, 512], P('op', 'sec'), may hold values from -0.25 to 0.25
- right_env: float32 [8, 32, 512, 512], P('op', 'sec'), may hold values from -0.09375 to 0.09375
- target: int32 [32], replicated, may hold values from 0 to 31, as said below
Outputs:
- sigma: float32 [32, 512, 512], P('sec', 'op')
The draws below stay inside these ranges and needn't reach their ends.
Inputs may be any that keep to these rules, and one draw needn't show every extreme that they name: target is a permutation of the 32 blocks; block r belongs to index r // 2 of sec; the block j of index d of sec (block d * 2 + j) lands on index (d + j + 1) mod (16) of sec, in a slot drawn from the seed.
All inputs are finite; a program needn't handle non-finite values.
Results may differ from the reference program's by a relative error of at most 0.00007.
Values sent between devices are 32-bit elements; how exact they have to be, the bound alone decides.
No kernel may reach another device: no remote copies, remote signals or barrier semaphores. Data moves between devices by JAX's collectives and lax.ppermute only.
A program may use at most 128 MiB of HBM per device.

```python
import jax
import jax.numpy as jnp
from jax import lax

B = 512
S_DEV = 2
NS = 32
K = 8


def draw_target(key, part):
    ndevice = NS // S_DEV
    scores = jax.random.randint(jax.random.fold_in(key, 7), (ndevice, S_DEV), 0, 1000000).astype(jnp.int32)
    scores = scores * S_DEV + jnp.arange(S_DEV, dtype=jnp.int32)[None, :]
    slots = jnp.argsort(scores, axis=1, stable=True).astype(jnp.int32)
    position = jnp.arange(NS, dtype=jnp.int32)
    source = position // S_DEV
    within = position % S_DEV
    dest = (source + within + 1) % ndevice
    return (dest * S_DEV + slots[dest, within]).astype(jnp.int32)


def level_of(own_key, dims, cuts, low, top_value):
    def one(dim, blocks):
        heights = jax.random.uniform(jax.random.fold_in(jax.random.fold_in(own_key, 6), dim), (blocks,), jnp.float32, low / len(cuts), top_value / len(cuts))
        return jnp.repeat(jnp.exp(heights), dims[dim] // blocks).reshape((-1,) + (1,) * (len(dims) - dim - 1))

    gain = one(*cuts[0])
    for cut in cuts[1:]:
        gain = gain * one(*cut)
    return gain


def centred(own_key, extent, width, bound, cuts=(), kind=jnp.bfloat16):
    result = width * jax.random.normal(own_key, extent, jnp.float32)
    if cuts:
        result = result * level_of(own_key, extent, cuts, -0.22, 0.18)
    return jnp.clip(result, -bound, bound).astype(kind)


def setup_inputs(seed: int = 0) -> dict:
    seeds = jax.random.split(jax.random.key(seed), 5)
    return {
        "psi": centred(seeds[0], (NS, B, B), 1.0, 6.0, ((0, 16),), jnp.float32),
        "left_env": centred(seeds[1], (K, NS, B, B), B ** -0.5, 0.25, ((0, 2), (1, 16)), jnp.float32),
        "right_env": centred(seeds[2], (K, NS, B, B), (B * K) ** -0.5, 0.09375, ((0, 2), (1, 16)), jnp.float32),
        "target": draw_target(jax.random.fold_in(seeds[4], 71), 0),
    }


def reference(psi, left_env, right_env, target):
    def one_block(index):
        left_part = jnp.einsum("kab,bc->kac", left_env[:, index], psi[index], precision=lax.Precision.HIGHEST)
        right_block = jnp.take(right_env, target[index], axis=1)
        return jnp.einsum("kac,kcd->ad", left_part, right_block, precision=lax.Precision.HIGHEST)

    blocks = lax.map(one_block, jnp.arange(NS, dtype=jnp.int32))
    return jnp.zeros_like(psi).at[target].set(blocks)
```

```python
import jax
import jax.numpy as jnp
from jax import lax
from jax.sharding import PartitionSpec as P


def product(first, second):
    return jnp.einsum("kab,bc->kac", first, second, precision=lax.Precision.HIGH)


def contract(first, second):
    return jnp.einsum("kac,kcd->ad", first, second, precision=lax.Precision.HIGH)


def per_device(psi, left_env, right_env, target):
    count = lax.axis_size("sec")
    me = lax.axis_index("sec")
    op = lax.axis_index("op")
    half = psi.shape[1] // 2

    def send(value, step, who=lambda d: True):
        pairs = [(d, (d + step(d)) % count) for d in range(count) if who(d)]
        return lax.ppermute(value, "sec", pairs)

    relayed = product(left_env[:, 0, half:], psi[0])
    hop = send(relayed, lambda d: (d ^ 2) - d, lambda d: d % 2 == 1)
    direct = product(left_env[:, 0, :half], psi[0])
    upper = send(direct, lambda d: 1)
    second = product(left_env[:, 1], psi[1])
    hop, upper, second, relayed = lax.optimization_barrier((hop, upper, second, relayed))

    whole = send(second, lambda d: 2)
    onward = jnp.where(me % 2 == 1, hop, relayed)
    lower = send(onward, lambda d: 1 if d % 2 == 0 else (-1 if d % 4 == 3 else 3))

    slots = [target[((me - j - 1) % count) * 2 + j] % 2 for j in range(2)]
    right = [lax.dynamic_index_in_dim(right_env, slot, 1, keepdims=False) for slot in slots]

    def both_terms(value):
        own = lax.dynamic_slice_in_dim(value, op * half, half, 0)
        other = lax.dynamic_slice_in_dim(value, (1 - op) * half, half, 0)
        return own + lax.ppermute(other, "op", [(0, 1), (1, 0)])

    sums = [
        both_terms(jnp.concatenate([contract(upper, right[0]), contract(lower, right[0])])),
        both_terms(contract(whole, right[1])),
    ]
    first = slots[0] == 0
    return jnp.stack([jnp.where(first, sums[0], sums[1]), jnp.where(first, sums[1], sums[0])])


def solution(mesh):
    return jax.shard_map(
        per_device,
        mesh=mesh,
        in_specs=(
            P("sec", None, None),
            P("op", "sec", None, None),
            P("op", "sec", None, None),
            P(),
        ),
        out_specs=P("sec", "op", None),
        check_vma=False,
    )
```

```python
import functools

import jax
import jax.numpy as jnp
from jax import lax
from jax.experimental import pallas as pl
from jax.experimental.pallas import tpu as pltpu
from jax.sharding import PartitionSpec as P


def split(value):
    high = value.astype(jnp.bfloat16)
    return high, (value - high.astype(jnp.float32)).astype(jnp.bfloat16)


def product_kernel(row_ref, left_ref, psi_ref, *refs, parts, pieces):
    outs, stack = refs[:-1], refs[-1]
    term = pl.program_id(0)
    width = psi_ref.shape[-1]

    @pl.when(term == 0)
    def _():
        high, low = split(psi_ref[0])
        stack[:width] = high
        stack[width : 2 * width] = high
        stack[2 * width :] = low

    high, low = split(left_ref[0, 0])
    result = jnp.dot(jnp.concatenate([high, low, high], axis=1), stack[...], preferred_element_type=jnp.float32)
    size = result.shape[0] // pieces
    first = 0
    for index, terms in enumerate(parts):

        @pl.when((term >= first) & (term < first + terms))
        def _():
            for piece in range(pieces):
                outs[index * pieces + piece][0] = result[piece * size : (piece + 1) * size]

        first += terms


def product(left_env, psi, block, row, rows, parts, first=0, pieces=1):
    width = psi.shape[-1]
    terms = sum(parts)
    size = rows // pieces
    starts = [sum(parts[:i]) for i in range(len(parts))]
    shapes, specs = [], []
    for start, count in zip(starts, parts):
        for _ in range(pieces):
            shapes.append(jax.ShapeDtypeStruct((count, size, width), jnp.float32))
            specs.append(
                pl.BlockSpec((1, size, width), lambda k, r, a=start, c=count: (jnp.clip(k - a, 0, c - 1), 0, 0))
            )
    return pl.pallas_call(
        functools.partial(product_kernel, parts=parts, pieces=pieces),
        out_shape=shapes,
        grid_spec=pltpu.PrefetchScalarGridSpec(
            num_scalar_prefetch=1,
            grid=(terms,),
            in_specs=[
                pl.BlockSpec((1, 1, rows, width), lambda k, r: (k + first, block, r[0], 0)),
                pl.BlockSpec((1, width, width), lambda k, r: (block, 0, 0)),
            ],
            out_specs=specs,
            scratch_shapes=[pltpu.VMEM((3 * width, width), jnp.bfloat16)],
        ),
        compiler_params=pltpu.CompilerParams(vmem_limit_bytes=48 * 2**20),
        cost_estimate=pl.CostEstimate(
            flops=6 * terms * rows * width * width, bytes_accessed=8 * terms * rows * width, transcendentals=0
        ),
    )(jnp.reshape(row, (1,)).astype(jnp.int32), left_env, psi)


def left_product(first, second):
    return jnp.einsum("kab,bc->kac", first, second, precision=lax.Precision.HIGH)


def contract(first, second):
    return jnp.einsum("kac,kcd->ad", first, second, precision=lax.Precision.HIGH)


def per_device(psi, left_env, right_env, target):
    count = lax.axis_size("sec")
    me = lax.axis_index("sec")
    op = lax.axis_index("op")
    half = psi.shape[1] // 2

    def send(value, step, who=lambda d: True):
        pairs = [(d, (d + step(d)) % count) for d in range(count) if who(d)]
        return lax.ppermute(value, "sec", pairs)

    terms = left_env.shape[0]
    upper_rows = half - 16
    lower = left_product(left_env[:, 0, upper_rows:], psi[0])
    hop = send(lower, lambda d: (d ^ 2) - d, lambda d: d % 2 == 1)
    upper = left_product(left_env[:, 0, :upper_rows], psi[0])
    direct = send(upper, lambda d: 1)
    onward = send(lower, lambda d: 1, lambda d: d % 2 == 0)

    chunks = product(left_env, psi, 1, 1 - op, half, (terms,))
    chunks += product(left_env, psi, 1, op, half, (terms - 1, 1))
    hop, direct, chunks = lax.optimization_barrier((hop, direct, chunks))
    others = send(chunks[0], lambda d: 2)
    most = send(chunks[1], lambda d: 2)
    relayed = send(hop, lambda d: -1 if d % 4 == 3 else 3, lambda d: d % 2 == 1)
    slots = [target[((me - j - 1) % count) * 2 + j] % 2 for j in range(2)]
    right = [lax.dynamic_index_in_dim(right_env, slot, 1, keepdims=False) for slot in slots]

    def exchange(value):
        return lax.ppermute(value, "op", [(0, 1), (1, 0)])

    others_sum = contract(others, right[1])
    others_sum, relayed = lax.optimization_barrier((others_sum, relayed))
    received = jnp.where(me % 2 == 1, onward, relayed)
    block = jnp.concatenate([contract(direct, right[0]), contract(received, right[0])])
    block, last = lax.optimization_barrier((block, chunks[2]))
    last = send(last, lambda d: 2)
    block_own = lax.dynamic_slice_in_dim(block, op * half, half, 0)
    block_other = lax.dynamic_slice_in_dim(block, (1 - op) * half, half, 0)
    done = block_own + exchange(block_other)
    early = contract(most, right[1][:-1]) + exchange(others_sum)
    done, early = lax.optimization_barrier((jnp.stack([done, done]), early))
    final = early + contract(last, right[1][-1:])
    return lax.dynamic_update_index_in_dim(done, final, slots[1], 0)


def solution(mesh):
    return jax.shard_map(
        per_device,
        mesh=mesh,
        in_specs=(
            P("sec", None, None),
            P("op", "sec", None, None),
            P("op", "sec", None, None),
            P(),
        ),
        out_specs=P("sec", "op", None),
        check_vma=False,
    )
```

```python
import functools

import jax
import jax.numpy as jnp
from jax import lax
from jax.experimental import pallas as pl
from jax.experimental.pallas import tpu as pltpu
from jax.sharding import PartitionSpec as P


def split(value):
    high = value.astype(jnp.bfloat16)
    return high, (value - high.astype(jnp.float32)).astype(jnp.bfloat16)


def product_kernel(place_ref, left_ref, psi_ref, *refs, parts, groups):
    outs = refs[: len(parts)]
    left, psi, stack, result, read, write = refs[len(parts) :]
    terms, rows, width = left.shape
    block = place_ref[0]
    start = pl.multiple_of(place_ref[1] * rows, rows)
    size = terms // groups
    psi_copy = pltpu.make_async_copy(psi_ref.at[block], psi, read.at[0])
    psi_copy.start()
    reads = []
    for group in range(groups):
        span = pl.ds(group * size, size)
        copy = pltpu.make_async_copy(left_ref.at[span, block, pl.ds(start, rows)], left.at[span], read.at[1 + group])
        copy.start()
        reads.append(copy)
    psi_copy.wait()
    high, low = split(psi[...])
    stack[:width] = high
    stack[width : 2 * width] = high
    stack[2 * width :] = low
    places = [(part, i) for part, count in enumerate(parts) for i in range(count)]
    writes = []
    for group in range(groups):
        reads[group].wait()
        span = slice(group * size, (group + 1) * size)
        high, low = split(left[span].reshape(size * rows, width))
        value = jnp.dot(jnp.concatenate([high, low, high], axis=1), stack[...], preferred_element_type=jnp.float32)
        result[span] = value.reshape(size, rows, width)
        for term in range(group * size, (group + 1) * size):
            part, i = places[term]
            copy = pltpu.make_async_copy(result.at[term], outs[part].at[i], write.at[term])
            copy.start()
            writes.append(copy)
    for copy in writes:
        copy.wait()


def product(left_env, psi, block, row, rows, parts):
    terms, _, _, width = left_env.shape
    groups = 2 if terms % 2 == 0 else 1
    place = jnp.stack([jnp.asarray(block, jnp.int32), jnp.asarray(row, jnp.int32)])
    return pl.pallas_call(
        functools.partial(product_kernel, parts=parts, groups=groups),
        out_shape=[jax.ShapeDtypeStruct((count, rows, width), jnp.float32) for count in parts],
        in_specs=[
            pl.BlockSpec(memory_space=pltpu.SMEM),
            pl.BlockSpec(memory_space=pltpu.HBM),
            pl.BlockSpec(memory_space=pltpu.HBM),
        ],
        out_specs=[pl.BlockSpec(memory_space=pl.ANY)] * len(parts),
        scratch_shapes=[
            pltpu.VMEM((terms, rows, width), jnp.float32),
            pltpu.VMEM((width, width), jnp.float32),
            pltpu.VMEM((3 * width, width), jnp.bfloat16),
            pltpu.VMEM((terms, rows, width), jnp.float32),
            pltpu.SemaphoreType.DMA((1 + groups,)),
            pltpu.SemaphoreType.DMA((terms,)),
        ],
        compiler_params=pltpu.CompilerParams(vmem_limit_bytes=32 * 2**20),
        cost_estimate=pl.CostEstimate(
            flops=6 * terms * rows * width * width, bytes_accessed=8 * terms * rows * width, transcendentals=0
        ),
    )(place, left_env, psi)


def contract(first, second):
    return jnp.einsum("kac,kcd->ad", first, second, precision=lax.Precision.HIGH)


def per_device(psi, left_env, right_env, target):
    count = lax.axis_size("sec")
    me = lax.axis_index("sec")
    own = lax.axis_index("op")
    other = 1 - own
    odd = me % 2
    half = psi.shape[1] // 2
    terms = left_env.shape[0]

    def send(value, step, who=lambda d: True):
        pairs = [(d, (d + step(d)) % count) for d in range(count) if who(d)]
        return lax.ppermute(value, "sec", pairs)

    def exchange(value):
        return lax.ppermute(value, "op", [(0, 1), (1, 0)])

    def after(*values):
        return lax.optimization_barrier(values)

    def right_of(slot):
        return lax.dynamic_index_in_dim(right_env, slot, 1, keepdims=False)

    slots = [target[((me - j - 1) % count) * 2 + j] % 2 for j in range(2)]
    right = [right_of(slot) for slot in slots]
    left_env, psi = (pltpu.with_memory_space_constraint(a, pltpu.HBM) for a in (left_env, psi))
    rows_of = functools.partial(product, left_env, psi, rows=half)

    (value,) = rows_of(1 - odd, other, parts=(terms,))
    first = send(value, lambda d: (d ^ 2) - d if d % 2 else 2)
    (value,) = rows_of(0, own, parts=(terms,))
    beside = send(value, lambda d: (d ^ 1) - d)
    (value,) = rows_of(1, jnp.where(odd == 1, other, own), parts=(terms,))
    (kept,) = rows_of(odd, jnp.where(odd == 1, own, other), parts=(terms,))

    first, value, kept = after(first, value, kept)
    second = send(value, lambda d: 2)
    relayed = send(
        jnp.where(odd == 1, first, kept), lambda d: 1 if d % 2 == 0 else (-1 if d % 4 == 3 else 3)
    )
    most = send(jnp.where(odd == 1, kept[:-1], beside[:-1]), lambda d: 2)
    others_1 = contract(jnp.where(odd == 1, second, first), right[1])
    others_1, relayed = after(others_1, relayed)
    others_0 = contract(relayed, right[0])
    others_0, last = after(others_0, jnp.where(odd == 1, kept[-1:], beside[-1:]))
    last = send(last, lambda d: 2)

    early = contract(jnp.where(odd == 1, beside, second), right_of(jnp.where(odd == 1, *slots)))
    late_slot = jnp.where(odd == 1, slots[1], slots[0])
    late_right = right_of(late_slot)
    swapped = [exchange(others_0), exchange(others_1)]
    early = early + jnp.where(odd == 1, *swapped)
    late = contract(most, late_right[:-1]) + jnp.where(odd == 1, swapped[1], swapped[0])
    out, late = after(jnp.stack([early, early]), late)
    final = late + contract(last, late_right[-1:])
    return lax.dynamic_update_index_in_dim(out, final, late_slot, 0)


def solution(mesh):
    return jax.shard_map(
        per_device,
        mesh=mesh,
        in_specs=(
            P("sec", None, None),
            P("op", "sec", None, None),
            P("op", "sec", None, None),
            P(),
        ),
        out_specs=P("sec", "op", None),
        check_vma=False,
    )
```

```python
import functools

import jax
import jax.numpy as jnp
from jax import lax
from jax.experimental import pallas as pl
from jax.experimental.pallas import tpu as pltpu
from jax.sharding import PartitionSpec as P


def split(value):
    high = value.astype(jnp.bfloat16)
    return high, (value - high.astype(jnp.float32)).astype(jnp.bfloat16)


def product_kernel(place_ref, left_ref, psi_ref, out_ref, left, psi, stack, result, read, write, *, first, groups):
    terms, rows, width = left.shape
    block = place_ref[0]
    start = pl.multiple_of(place_ref[1] * rows, rows)
    size = terms // groups
    psi_copy = pltpu.make_async_copy(psi_ref.at[block], psi, read.at[0])
    psi_copy.start()
    reads = []
    for group in range(groups):
        span = pl.ds(group * size, size)
        source = left_ref.at[pl.ds(first + group * size, size), block, pl.ds(start, rows)]
        copy = pltpu.make_async_copy(source, left.at[span], read.at[1 + group])
        copy.start()
        reads.append(copy)
    psi_copy.wait()
    high, low = split(psi[...])
    stack[:width] = high
    stack[width : 2 * width] = high
    stack[2 * width :] = low
    writes = []
    for group in range(groups):
        reads[group].wait()
        span = slice(group * size, (group + 1) * size)
        high, low = split(left[span].reshape(size * rows, width))
        value = jnp.dot(jnp.concatenate([high, low, high], axis=1), stack[...], preferred_element_type=jnp.float32)
        result[span] = value.reshape(size, rows, width)
        copy = pltpu.make_async_copy(result.at[pl.ds(group * size, size)], out_ref.at[pl.ds(group * size, size)], write.at[group])
        copy.start()
        writes.append(copy)
    for copy in writes:
        copy.wait()


def product(left_env, psi, block, row, rows, first=0, terms=None, cost=1):
    width = psi.shape[-1]
    terms = terms or left_env.shape[0] - first
    groups = 2 if terms % 2 == 0 else terms
    place = jnp.stack([jnp.asarray(block, jnp.int32), jnp.asarray(row, jnp.int32)])
    return pl.pallas_call(
        functools.partial(product_kernel, first=first, groups=groups),
        out_shape=jax.ShapeDtypeStruct((terms, rows, width), jnp.float32),
        in_specs=[
            pl.BlockSpec(memory_space=pltpu.SMEM),
            pl.BlockSpec(memory_space=pltpu.HBM),
            pl.BlockSpec(memory_space=pltpu.HBM),
        ],
        out_specs=pl.BlockSpec(memory_space=pl.ANY),
        scratch_shapes=[
            pltpu.VMEM((terms, rows, width), jnp.float32),
            pltpu.VMEM((width, width), jnp.float32),
            pltpu.VMEM((3 * width, width), jnp.bfloat16),
            pltpu.VMEM((terms, rows, width), jnp.float32),
            pltpu.SemaphoreType.DMA((1 + groups,)),
            pltpu.SemaphoreType.DMA((groups,)),
        ],
        compiler_params=pltpu.CompilerParams(vmem_limit_bytes=32 * 2**20),
        cost_estimate=pl.CostEstimate(
            flops=6 * terms * rows * width * width * cost, bytes_accessed=8 * terms * rows * width, transcendentals=0
        ),
    )(place, left_env, psi)


def contract(first, second):
    return jnp.einsum("kac,kcd->ad", first, second, precision=lax.Precision.HIGH)


def per_device(psi, left_env, right_env, target):
    count = lax.axis_size("sec")
    me = lax.axis_index("sec")
    own = lax.axis_index("op")
    other = 1 - own
    odd = me % 2
    half = psi.shape[1] // 2
    terms = left_env.shape[0]

    def send(value, step, who=lambda d: True):
        pairs = [(d, (d + step(d)) % count) for d in range(count) if who(d)]
        return lax.ppermute(value, "sec", pairs)

    def exchange(value):
        return lax.ppermute(value, "op", [(0, 1), (1, 0)])

    def after(*values):
        return lax.optimization_barrier(values)

    def right_of(slot):
        return lax.dynamic_index_in_dim(right_env, slot, 1, keepdims=False)

    slots = [target[((me - j - 1) % count) * 2 + j] % 2 for j in range(2)]
    right = [right_of(slot) for slot in slots]
    left_env, psi = (pltpu.with_memory_space_constraint(a, pltpu.HBM) for a in (left_env, psi))
    rows_of = functools.partial(product, left_env, psi, rows=half)

    value = rows_of(1 - odd, other)
    first = send(value, lambda d: (d ^ 2) - d if d % 2 else 2)
    value = rows_of(0, own)
    beside = send(value, lambda d: (d ^ 1) - d)
    value = rows_of(1, jnp.where(odd == 1, other, own))
    kept = rows_of(odd, jnp.where(odd == 1, own, other))

    first, value, kept = after(first, value, kept)
    second = send(value, lambda d: 2)
    relayed = send(
        jnp.where(odd == 1, first, kept), lambda d: 1 if d % 2 == 0 else (-1 if d % 4 == 3 else 3)
    )
    most = send(jnp.where(odd == 1, kept[:-1], beside[:-1]), lambda d: 2)
    others_1 = contract(jnp.where(odd == 1, second, first), right[1])
    others_1, relayed = after(others_1, relayed)
    others_0 = contract(relayed, right[0])
    others_0, last = after(others_0, jnp.where(odd == 1, kept[-1:], beside[-1:]))
    last = send(last, lambda d: 2)

    early = contract(jnp.where(odd == 1, beside, second), right_of(jnp.where(odd == 1, *slots)))
    late_slot = jnp.where(odd == 1, slots[1], slots[0])
    late_right = right_of(late_slot)
    swapped = [exchange(others_0), exchange(others_1)]
    early = early + jnp.where(odd == 1, *swapped)
    late = contract(most, late_right[:-1]) + jnp.where(odd == 1, swapped[1], swapped[0])
    out, late, late_right = after(jnp.stack([early, early]), late, late_right[-1])
    final = late + jnp.dot(last[0], late_right, precision=lax.Precision.HIGH)
    return lax.dynamic_update_index_in_dim(out, final, late_slot, 0)


def solution(mesh):
    return jax.shard_map(
        per_device,
        mesh=mesh,
        in_specs=(
            P("sec", None, None),
            P("op", "sec", None, None),
            P("op", "sec", None, None),
            P(),
        ),
        out_specs=P("sec", "op", None),
        check_vma=False,
    )
```

```python
import functools

import jax
import jax.numpy as jnp
from jax import lax
from jax.experimental import pallas as pl
from jax.experimental.pallas import tpu as pltpu
from jax.sharding import PartitionSpec as P


def split(value):
    high = value.astype(jnp.bfloat16)
    return high, (value - high.astype(jnp.float32)).astype(jnp.bfloat16)


def product_kernel(left_ref, psi_ref, out_ref, left, psi, stack, result, read, write, *, place, groups):
    terms, rows, width = left.shape
    block, row = place(lax.rem(lax.axis_index("sec"), 2), lax.axis_index("op"))
    start = pl.multiple_of(row * rows, rows)
    size = terms // groups
    psi_copy = pltpu.make_async_copy(psi_ref.at[block], psi, read.at[0])
    psi_copy.start()
    reads = []
    for group in range(groups):
        span = pl.ds(group * size, size)
        source = left_ref.at[pl.ds(group * size, size), block, pl.ds(start, rows)]
        copy = pltpu.make_async_copy(source, left.at[span], read.at[1 + group])
        copy.start()
        reads.append(copy)
    psi_copy.wait()
    high, low = split(psi[...])
    stack[:width] = high
    stack[width : 2 * width] = high
    stack[2 * width :] = low
    writes = []
    for group in range(groups):
        reads[group].wait()
        span = slice(group * size, (group + 1) * size)
        high, low = split(left[span].reshape(size * rows, width))
        value = jnp.dot(jnp.concatenate([high, low, high], axis=1), stack[...], preferred_element_type=jnp.float32)
        result[span] = value.reshape(size, rows, width)
        copy = pltpu.make_async_copy(result.at[pl.ds(group * size, size)], out_ref.at[pl.ds(group * size, size)], write.at[group])
        copy.start()
        writes.append(copy)
    for copy in writes:
        copy.wait()


def product(left_env, psi, place):
    width = psi.shape[-1]
    rows = width // 2
    terms = left_env.shape[0]
    groups = 2 if terms % 2 == 0 else 1
    return pl.pallas_call(
        functools.partial(product_kernel, place=place, groups=groups),
        out_shape=jax.ShapeDtypeStruct((terms, rows, width), jnp.float32),
        in_specs=[
            pl.BlockSpec(memory_space=pltpu.HBM),
            pl.BlockSpec(memory_space=pltpu.HBM),
        ],
        out_specs=pl.BlockSpec(memory_space=pl.ANY),
        scratch_shapes=[
            pltpu.VMEM((terms, rows, width), jnp.float32),
            pltpu.VMEM((width, width), jnp.float32),
            pltpu.VMEM((3 * width, width), jnp.bfloat16),
            pltpu.VMEM((terms, rows, width), jnp.float32),
            pltpu.SemaphoreType.DMA((1 + groups,)),
            pltpu.SemaphoreType.DMA((groups,)),
        ],
        compiler_params=pltpu.CompilerParams(vmem_limit_bytes=32 * 2**20),
        cost_estimate=pl.CostEstimate(
            flops=6 * terms * rows * width * width, bytes_accessed=8 * terms * rows * width, transcendentals=0
        ),
    )(left_env, psi)


def contract(first, second):
    return jnp.einsum("kac,kcd->ad", first, second, precision=lax.Precision.HIGH)


def per_device(psi, left_env, right_env, target):
    count = lax.axis_size("sec")
    me = lax.axis_index("sec")
    odd = me % 2

    def send(value, step, who=lambda d: True):
        pairs = [(d, (d + step(d)) % count) for d in range(count) if who(d)]
        return lax.ppermute(value, "sec", pairs)

    def exchange(value):
        return lax.ppermute(value, "op", [(0, 1), (1, 0)])

    def after(*values):
        return lax.optimization_barrier(values)

    def right_of(slot):
        return lax.dynamic_index_in_dim(right_env, slot, 1, keepdims=False)

    slots = [target[((me - j - 1) % count) * 2 + j] % 2 for j in range(2)]
    right = [right_of(slot) for slot in slots]
    left_env, psi = (pltpu.with_memory_space_constraint(a, pltpu.HBM) for a in (left_env, psi))
    rows_of = functools.partial(product, left_env, psi)

    value = rows_of(lambda odd, own: (1 - odd, 1 - own))
    first = send(value, lambda d: (d ^ 2) - d if d % 2 else 2)
    value = rows_of(lambda odd, own: (0, own))
    beside = send(value, lambda d: (d ^ 1) - d)
    value = rows_of(lambda odd, own: (1, jnp.where(odd == 1, 1 - own, own)))
    kept = rows_of(lambda odd, own: (odd, jnp.where(odd == 1, own, 1 - own)))

    first, value, kept = after(first, value, kept)
    second = send(value, lambda d: 2)
    relayed = send(
        jnp.where(odd == 1, first, kept), lambda d: 1 if d % 2 == 0 else (-1 if d % 4 == 3 else 3)
    )
    most = send(jnp.where(odd == 1, kept[:-1], beside[:-1]), lambda d: 2)
    others_1 = contract(jnp.where(odd == 1, second, first), right[1])
    others_1, relayed = after(others_1, relayed)
    others_0 = contract(relayed, right[0])
    others_0, last = after(others_0, jnp.where(odd == 1, kept[-1:], beside[-1:]))
    last = send(last, lambda d: 2)

    early = contract(jnp.where(odd == 1, beside, second), right_of(jnp.where(odd == 1, *slots)))
    late_slot = jnp.where(odd == 1, slots[1], slots[0])
    late_right = right_of(late_slot)
    swapped = [exchange(others_0), exchange(others_1)]
    early = early + jnp.where(odd == 1, *swapped)
    late = contract(most, late_right[:-1]) + jnp.where(odd == 1, swapped[1], swapped[0])
    out, late, late_right = after(jnp.stack([early, early]), late, late_right[-1])
    final = late + jnp.dot(last[0], late_right, precision=lax.Precision.HIGH)
    return lax.dynamic_update_index_in_dim(out, final, late_slot, 0)


def solution(mesh):
    return jax.shard_map(
        per_device,
        mesh=mesh,
        in_specs=(
            P("sec", None, None),
            P("op", "sec", None, None),
            P("op", "sec", None, None),
            P(),
        ),
        out_specs=P("sec", "op", None),
        check_vma=False,
    )
```

```python
import functools

import jax
import jax.numpy as jnp
from jax import lax
from jax.experimental import pallas as pl
from jax.experimental.pallas import tpu as pltpu
from jax.sharding import PartitionSpec as P


def split(value):
    high = value.astype(jnp.bfloat16)
    return high, (value - high.astype(jnp.float32)).astype(jnp.bfloat16)


def product_kernel(left_ref, psi_ref, *refs, place, first, groups):
    count = sum(1 for _, _, fresh in groups if fresh)
    outs = refs[:count]
    left, psi, stack, result, read, write = refs[count:]
    _, rows, width = left.shape
    block, row = place(lax.rem(lax.axis_index("sec"), 2), lax.axis_index("op"))
    start = pl.multiple_of(row * rows, rows)
    psi_copy = pltpu.make_async_copy(psi_ref.at[block], psi, read.at[0])
    psi_copy.start()
    reads = []
    for index, (at, size, _) in enumerate(groups):
        source = left_ref.at[pl.ds(first + at, size), block, pl.ds(start, rows)]
        copy = pltpu.make_async_copy(source, left.at[pl.ds(at, size)], read.at[1 + index])
        copy.start()
        reads.append(copy)
    psi_copy.wait()
    high, low = split(psi[...])
    stack[:width] = high
    stack[width : 2 * width] = high
    stack[2 * width :] = low
    writes = []
    out, base = -1, 0
    for index, (at, size, fresh) in enumerate(groups):
        if fresh:
            out, base = out + 1, at
        reads[index].wait()
        high, low = split(left[at : at + size].reshape(size * rows, width))
        value = jnp.dot(jnp.concatenate([high, low, high], axis=1), stack[...], preferred_element_type=jnp.float32)
        result[at : at + size] = value.reshape(size, rows, width)
        target = outs[out].at[pl.ds(at - base, size)]
        copy = pltpu.make_async_copy(result.at[pl.ds(at, size)], target, write.at[index])
        copy.start()
        writes.append(copy)
    for copy in writes:
        copy.wait()


def product(left_env, psi, place, first=0, parts=None, cost=1):
    width = psi.shape[-1]
    rows = width // 2
    parts = parts or (left_env.shape[0] - first,)
    terms = sum(parts)
    groups, at = [], 0
    for part in parts:
        for size, fresh in ((part - part // 2, True), (part // 2, False)):
            if size:
                groups.append((at, size, fresh))
                at += size
    return pl.pallas_call(
        functools.partial(product_kernel, place=place, first=first, groups=groups),
        out_shape=[jax.ShapeDtypeStruct((part, rows, width), jnp.float32) for part in parts],
        in_specs=[pl.BlockSpec(memory_space=pltpu.HBM)] * 2,
        out_specs=[pl.BlockSpec(memory_space=pl.ANY)] * len(parts),
        scratch_shapes=[
            pltpu.VMEM((terms, rows, width), jnp.float32),
            pltpu.VMEM((width, width), jnp.float32),
            pltpu.VMEM((3 * width, width), jnp.bfloat16),
            pltpu.VMEM((terms, rows, width), jnp.float32),
            pltpu.SemaphoreType.DMA((1 + len(groups),)),
            pltpu.SemaphoreType.DMA((len(groups),)),
        ],
        compiler_params=pltpu.CompilerParams(vmem_limit_bytes=32 * 2**20),
        cost_estimate=pl.CostEstimate(
            flops=6 * terms * rows * width * width * cost, bytes_accessed=8 * terms * rows * width, transcendentals=0
        ),
    )(left_env, psi)


def contract(first, second):
    return jnp.einsum("kac,kcd->ad", first, second, precision=lax.Precision.HIGH)


def per_device(psi, left_env, right_env, target):
    count = lax.axis_size("sec")
    me = lax.axis_index("sec")
    odd = me % 2

    def send(value, step, who=lambda d: True):
        pairs = [(d, (d + step(d)) % count) for d in range(count) if who(d)]
        return lax.ppermute(value, "sec", pairs)

    def exchange(value):
        return lax.ppermute(value, "op", [(0, 1), (1, 0)])

    def after(*values):
        return lax.optimization_barrier(values)

    def right_of(slot):
        return lax.dynamic_index_in_dim(right_env, slot, 1, keepdims=False)

    slots = [target[((me - j - 1) % count) * 2 + j] % 2 for j in range(2)]
    right = [right_of(slot) for slot in slots]
    left_env, psi = (pltpu.with_memory_space_constraint(a, pltpu.HBM) for a in (left_env, psi))
    rows_of = functools.partial(product, left_env, psi)

    terms = left_env.shape[0]
    (value,) = rows_of(lambda odd, own: (1 - odd, 1 - own), parts=(1,))
    ahead = send(value, lambda d: (d ^ 2) - d if d % 2 else 2)
    near, near_last = rows_of(lambda odd, own: (0, own), parts=(terms - 1, 1))
    beside = send(near, lambda d: (d ^ 1) - d)
    (value,) = rows_of(lambda odd, own: (1 - odd, 1 - own), first=1)
    first = send(value, lambda d: (d ^ 2) - d if d % 2 else 2)
    ahead, psi = after(ahead, psi)
    (value,) = product(left_env, psi, lambda odd, own: (1, jnp.where(odd == 1, 1 - own, own)), cost=100)
    beside, psi = after(beside, psi)
    kept, kept_last = product(
        left_env, psi, lambda odd, own: (odd, jnp.where(odd == 1, own, 1 - own)), parts=(terms - 1, 1), cost=100
    )

    first, value, kept, kept_last, near_last = after(first, value, kept, kept_last, near_last)
    second = send(value, lambda d: 2)
    first = jnp.concatenate([ahead, first])
    beside_last = send(near_last, lambda d: (d ^ 1) - d)
    relayed = send(
        jnp.where(odd == 1, first, jnp.concatenate([kept, kept_last])),
        lambda d: 1 if d % 2 == 0 else (-1 if d % 4 == 3 else 3),
    )
    most = send(jnp.where(odd == 1, kept, beside), lambda d: 2)
    others_1 = contract(jnp.where(odd == 1, second, first), right[1])
    others_1, relayed = after(others_1, relayed)
    others_0 = contract(relayed, right[0])
    others_0, last = after(others_0, jnp.where(odd == 1, kept_last, beside_last))
    last = send(last, lambda d: 2)

    beside = jnp.concatenate([beside, beside_last])
    early = contract(jnp.where(odd == 1, beside, second), right_of(jnp.where(odd == 1, *slots)))
    late_slot = jnp.where(odd == 1, slots[1], slots[0])
    late_right = right_of(late_slot)
    swapped = [exchange(others_0), exchange(others_1)]
    early = early + jnp.where(odd == 1, *swapped)
    late = contract(most, late_right[:-1]) + jnp.where(odd == 1, swapped[1], swapped[0])
    out, late, late_right = after(jnp.stack([early, early]), late, late_right[-1])
    final = late + jnp.dot(last[0], late_right, precision=lax.Precision.HIGH)
    return lax.dynamic_update_index_in_dim(out, final, late_slot, 0)


def solution(mesh):
    return jax.shard_map(
        per_device,
        mesh=mesh,
        in_specs=(
            P("sec", None, None),
            P("op", "sec", None, None),
            P("op", "sec", None, None),
            P(),
        ),
        out_specs=P("sec", "op", None),
        check_vma=False,
    )
```

```python
import functools

import jax
import jax.numpy as jnp
from jax import lax
from jax.experimental import pallas as pl
from jax.experimental.pallas import tpu as pltpu
from jax.sharding import PartitionSpec as P


def split(value):
    high = value.astype(jnp.bfloat16)
    return high, (value - high.astype(jnp.float32)).astype(jnp.bfloat16)


def product_kernel(left_ref, psi_ref, *refs, place, first, groups):
    count = sum(1 for _, _, fresh in groups if fresh)
    outs = refs[:count]
    left, psi, stack, result, read, write = refs[count:]
    _, rows, width = left.shape
    block, row = place(lax.rem(lax.axis_index("sec"), 2), lax.axis_index("op"))
    start = pl.multiple_of(row * rows, rows)
    psi_copy = pltpu.make_async_copy(psi_ref.at[block], psi, read.at[0])
    psi_copy.start()
    reads = []
    for index, (at, size, _) in enumerate(groups):
        source = left_ref.at[pl.ds(first + at, size), block, pl.ds(start, rows)]
        copy = pltpu.make_async_copy(source, left.at[pl.ds(at, size)], read.at[1 + index])
        copy.start()
        reads.append(copy)
    psi_copy.wait()
    high, low = split(psi[...])
    stack[:width] = high
    stack[width : 2 * width] = high
    stack[2 * width :] = low
    writes = []
    out, base = -1, 0
    for index, (at, size, fresh) in enumerate(groups):
        if fresh:
            out, base = out + 1, at
        reads[index].wait()
        high, low = split(left[at : at + size].reshape(size * rows, width))
        value = jnp.dot(jnp.concatenate([high, low, high], axis=1), stack[...], preferred_element_type=jnp.float32)
        result[at : at + size] = value.reshape(size, rows, width)
        target = outs[out].at[pl.ds(at - base, size)]
        copy = pltpu.make_async_copy(result.at[pl.ds(at, size)], target, write.at[index])
        copy.start()
        writes.append(copy)
    for copy in writes:
        copy.wait()


def product(left_env, psi, place, first=0, parts=None, cost=1):
    width = psi.shape[-1]
    rows = width // 2
    parts = parts or (left_env.shape[0] - first,)
    terms = sum(parts)
    groups, at = [], 0
    for part in parts:
        for size, fresh in ((part - part // 2, True), (part // 2, False)):
            if size:
                groups.append((at, size, fresh))
                at += size
    return pl.pallas_call(
        functools.partial(product_kernel, place=place, first=first, groups=groups),
        out_shape=[jax.ShapeDtypeStruct((part, rows, width), jnp.float32) for part in parts],
        in_specs=[pl.BlockSpec(memory_space=pltpu.HBM)] * 2,
        out_specs=[pl.BlockSpec(memory_space=pl.ANY)] * len(parts),
        scratch_shapes=[
            pltpu.VMEM((terms, rows, width), jnp.float32),
            pltpu.VMEM((width, width), jnp.float32),
            pltpu.VMEM((3 * width, width), jnp.bfloat16),
            pltpu.VMEM((terms, rows, width), jnp.float32),
            pltpu.SemaphoreType.DMA((1 + len(groups),)),
            pltpu.SemaphoreType.DMA((len(groups),)),
        ],
        compiler_params=pltpu.CompilerParams(vmem_limit_bytes=32 * 2**20),
        cost_estimate=pl.CostEstimate(
            flops=6 * terms * rows * width * width * cost, bytes_accessed=8 * terms * rows * width, transcendentals=0
        ),
    )(left_env, psi)


def contract(first, second):
    return jnp.einsum("kac,kcd->ad", first, second, precision=lax.Precision.HIGH)


def per_device(psi, left_env, right_env, target):
    count = lax.axis_size("sec")
    me = lax.axis_index("sec")
    odd = me % 2

    def send(value, step, who=lambda d: True):
        pairs = [(d, (d + step(d)) % count) for d in range(count) if who(d)]
        return lax.ppermute(value, "sec", pairs)

    def exchange(value):
        return lax.ppermute(value, "op", [(0, 1), (1, 0)])

    def after(*values):
        return lax.optimization_barrier(values)

    def right_of(slot):
        return lax.dynamic_index_in_dim(right_env, slot, 1, keepdims=False)

    slots = [target[((me - j - 1) % count) * 2 + j] % 2 for j in range(2)]
    right = [right_of(slot) for slot in slots]
    left_env, psi = (pltpu.with_memory_space_constraint(a, pltpu.HBM) for a in (left_env, psi))
    rows_of = functools.partial(product, left_env, psi)

    terms = left_env.shape[0]
    (value,) = rows_of(lambda odd, own: (1 - odd, 1 - own), parts=(1,))
    ahead = send(value, lambda d: (d ^ 2) - d if d % 2 else 2)
    (value,) = rows_of(lambda odd, own: (0, own))
    value, later = after(value, psi)
    beside = send(value, lambda d: (d ^ 1) - d)
    (value,) = product(left_env, later, lambda odd, own: (1 - odd, 1 - own), first=1)
    first = send(value, lambda d: (d ^ 2) - d if d % 2 else 2)
    ahead, psi = after(ahead, psi)
    (value,) = product(left_env, psi, lambda odd, own: (1, jnp.where(odd == 1, 1 - own, own)), cost=100)
    (kept,) = product(left_env, psi, lambda odd, own: (odd, jnp.where(odd == 1, own, 1 - own)), cost=1)

    first, value, kept = after(first, value, kept)
    second = send(value, lambda d: 2)
    first = jnp.concatenate([ahead, first])
    relayed = send(
        jnp.where(odd == 1, first, kept),
        lambda d: 1 if d % 2 == 0 else (-1 if d % 4 == 3 else 3),
    )
    most = send(jnp.where(odd == 1, kept[:-1], beside[:-1]), lambda d: 2)
    others_1 = contract(jnp.where(odd == 1, second, first), right[1])
    others_1, relayed = after(others_1, relayed)
    others_0 = contract(relayed, right[0])
    others_0, last = after(others_0, jnp.where(odd == 1, kept[-1:], beside[-1:]))
    last = send(last, lambda d: 2)

    early = contract(jnp.where(odd == 1, beside, second), right_of(jnp.where(odd == 1, *slots)))
    late_slot = jnp.where(odd == 1, slots[1], slots[0])
    late_right = right_of(late_slot)
    swapped = [exchange(others_0), exchange(others_1)]
    early = early + jnp.where(odd == 1, *swapped)
    late = contract(most, late_right[:-1]) + jnp.where(odd == 1, swapped[1], swapped[0])
    out, late, late_right = after(jnp.stack([early, early]), late, late_right[-1])
    final = late + jnp.dot(last[0], late_right, precision=lax.Precision.HIGH)
    return lax.dynamic_update_index_in_dim(out, final, late_slot, 0)


def solution(mesh):
    return jax.shard_map(
        per_device,
        mesh=mesh,
        in_specs=(
            P("sec", None, None),
            P("op", "sec", None, None),
            P("op", "sec", None, None),
            P(),
        ),
        out_specs=P("sec", "op", None),
        check_vma=False,
    )
```

```python
import functools

import jax
import jax.numpy as jnp
from jax import lax
from jax.experimental import pallas as pl
from jax.experimental.pallas import tpu as pltpu
from jax.sharding import PartitionSpec as P


def split(value):
    high = value.astype(jnp.bfloat16)
    return high, (value - high.astype(jnp.float32)).astype(jnp.bfloat16)


def product_kernel(left_ref, psi_ref, *refs, place, first, groups):
    count = sum(1 for _, _, fresh in groups if fresh)
    outs = refs[:count]
    left, psi, stack, result, read, write = refs[count:]
    _, rows, width = left.shape
    block, row = place(lax.rem(lax.axis_index("sec"), 2), lax.axis_index("op"))
    start = pl.multiple_of(row * rows, rows)
    psi_copy = pltpu.make_async_copy(psi_ref.at[block], psi, read.at[0])
    psi_copy.start()
    reads = []
    for index, (at, size, _) in enumerate(groups):
        source = left_ref.at[pl.ds(first + at, size), block, pl.ds(start, rows)]
        copy = pltpu.make_async_copy(source, left.at[pl.ds(at, size)], read.at[1 + index])
        copy.start()
        reads.append(copy)
    psi_copy.wait()
    high, low = split(psi[...])
    stack[:width] = high
    stack[width : 2 * width] = high
    stack[2 * width :] = low
    writes = []
    out, base = -1, 0
    for index, (at, size, fresh) in enumerate(groups):
        if fresh:
            out, base = out + 1, at
        reads[index].wait()
        high, low = split(left[at : at + size].reshape(size * rows, width))
        value = jnp.dot(jnp.concatenate([high, low, high], axis=1), stack[...], preferred_element_type=jnp.float32)
        result[at : at + size] = value.reshape(size, rows, width)
        target = outs[out].at[pl.ds(at - base, size)]
        copy = pltpu.make_async_copy(result.at[pl.ds(at, size)], target, write.at[index])
        copy.start()
        writes.append(copy)
    for copy in writes:
        copy.wait()


def product(left_env, psi, place, first=0, parts=None, cost=1):
    width = psi.shape[-1]
    rows = width // 2
    parts = parts or (left_env.shape[0] - first,)
    terms = sum(parts)
    groups, at = [], 0
    for part in parts:
        for size, fresh in ((part - part // 2, True), (part // 2, False)):
            if size:
                groups.append((at, size, fresh))
                at += size
    return pl.pallas_call(
        functools.partial(product_kernel, place=place, first=first, groups=groups),
        out_shape=[jax.ShapeDtypeStruct((part, rows, width), jnp.float32) for part in parts],
        in_specs=[pl.BlockSpec(memory_space=pltpu.HBM)] * 2,
        out_specs=[pl.BlockSpec(memory_space=pl.ANY)] * len(parts),
        scratch_shapes=[
            pltpu.VMEM((terms, rows, width), jnp.float32),
            pltpu.VMEM((width, width), jnp.float32),
            pltpu.VMEM((3 * width, width), jnp.bfloat16),
            pltpu.VMEM((terms, rows, width), jnp.float32),
            pltpu.SemaphoreType.DMA((1 + len(groups),)),
            pltpu.SemaphoreType.DMA((len(groups),)),
        ],
        compiler_params=pltpu.CompilerParams(vmem_limit_bytes=32 * 2**20),
        cost_estimate=pl.CostEstimate(
            flops=6 * terms * rows * width * width * cost, bytes_accessed=8 * terms * rows * width, transcendentals=0
        ),
    )(left_env, psi)


def contract(first, second):
    return jnp.einsum("kac,kcd->ad", first, second, precision=lax.Precision.HIGH)


def per_device(psi, left_env, right_env, target):
    count = lax.axis_size("sec")
    me = lax.axis_index("sec")
    odd = me % 2

    def send(value, step, who=lambda d: True):
        pairs = [(d, (d + step(d)) % count) for d in range(count) if who(d)]
        return lax.ppermute(value, "sec", pairs)

    def exchange(value):
        return lax.ppermute(value, "op", [(0, 1), (1, 0)])

    def after(*values):
        return lax.optimization_barrier(values)

    def right_of(slot):
        return lax.dynamic_index_in_dim(right_env, slot, 1, keepdims=False)

    slots = [target[((me - j - 1) % count) * 2 + j] % 2 for j in range(2)]
    right = [right_of(slot) for slot in slots]
    left_env, psi = (pltpu.with_memory_space_constraint(a, pltpu.HBM) for a in (left_env, psi))
    rows_of = functools.partial(product, left_env, psi)

    terms = left_env.shape[0]
    (value,) = rows_of(lambda odd, own: (1 - odd, 1 - own), parts=(1,))
    ahead = send(value, lambda d: (d ^ 2) - d if d % 2 else 2)
    (value,) = rows_of(lambda odd, own: (0, own))
    value, later = after(value, psi)
    beside = send(value, lambda d: (d ^ 1) - d)
    (value,) = product(left_env, later, lambda odd, own: (1 - odd, 1 - own), first=1)
    first = send(value, lambda d: (d ^ 2) - d if d % 2 else 2)
    ahead, psi = after(ahead, psi)
    (value,) = product(left_env, psi, lambda odd, own: (1, jnp.where(odd == 1, 1 - own, own)), cost=100)
    (kept,) = product(left_env, psi, lambda odd, own: (odd, jnp.where(odd == 1, own, 1 - own)), cost=1)

    onward = send(kept, lambda d: 1, lambda d: d % 2 == 0)
    second_even = send(value, lambda d: 2, lambda d: d % 2 == 0)
    first, gated = after(first, value)
    second_odd = send(gated, lambda d: 2, lambda d: d % 2 == 1)
    first = jnp.concatenate([ahead, first])
    hop = send(first, lambda d: -1 if d % 4 == 3 else 3, lambda d: d % 2 == 1)
    most = send(jnp.where(odd == 1, kept[:-1], beside[:-1]), lambda d: 2)
    second = jnp.where(odd == 1, second_odd, second_even)
    relayed = jnp.where(odd == 1, onward, hop)
    others_1 = contract(jnp.where(odd == 1, second, first), right[1])
    others_1, relayed = after(others_1, relayed)
    others_0 = contract(relayed, right[0])
    others_0, last = after(others_0, jnp.where(odd == 1, kept[-1:], beside[-1:]))
    last = send(last, lambda d: 2)

    early = contract(jnp.where(odd == 1, beside, second), right_of(jnp.where(odd == 1, *slots)))
    late_slot = jnp.where(odd == 1, slots[1], slots[0])
    late_right = right_of(late_slot)
    swapped = [exchange(others_0), exchange(others_1)]
    early = early + jnp.where(odd == 1, *swapped)
    late = contract(most, late_right[:-1]) + jnp.where(odd == 1, swapped[1], swapped[0])
    out, late, late_right = after(jnp.stack([early, early]), late, late_right[-1])
    final = late + jnp.dot(last[0], late_right, precision=lax.Precision.HIGH)
    return lax.dynamic_update_index_in_dim(out, final, late_slot, 0)


def solution(mesh):
    return jax.shard_map(
        per_device,
        mesh=mesh,
        in_specs=(
            P("sec", None, None),
            P("op", "sec", None, None),
            P("op", "sec", None, None),
            P(),
        ),
        out_specs=P("sec", "op", None),
        check_vma=False,
    )
```
